32 devices in a mesh: grp: 2 (over y), row: 4 (over z), col: 2 (over x), hd: 2 (over core).
Axes of the slice: x: 2, y: 2, z: 4, core: 2. Of those that a mesh axis runs over, the one named last changes fastest.
Arguments:
- queries: bfloat16 [8, 64, 32, 1536], P('grp', 'row', 'col', 'hd'), parts along dimension 0, may hold values from -6 to 6
- keys: bfloat16 [8, 64, 32, 1536], P('grp', 'row', 'col', 'hd'), parts along dimension 0, may hold values from -6 to 6
- values: bfloat16 [8, 64, 32, 1536], P('grp', 'row', 'col', 'hd'), parts along dimension 0, may hold values from -6 to 6
- labels: int32 [8, 4, 2], P('grp'), parts along dimension 0, may hold values from 0 to 2
- pad_rows: int32 [2], P('grp'), parts along dimension 0, may hold values from 0 to 31
- pad_cols: int32 [2], P('grp'), parts along dimension 0, may hold values from 0 to 31
Outputs:
- attended: bfloat16 [8, 64, 32, 1536], P('grp', 'row', 'col', 'hd'), parts along dimension 0
The draws below stay inside these ranges and needn't reach their ends.
There are 2 independent parts, one for each index of `grp`. The reference program is written for one: setup_inputs(seed, part) draws one part's arguments, and reference() takes and returns one part's arrays. A program takes and returns all parts, laid end to end along the dimension named above; each array names one. Nothing has to cross between parts.
All inputs are finite; a program needn't handle non-finite values.
Results may differ from the reference program's by a relative error of at most 0.008.
Values may be sent and summed in bfloat16 or wider, within the bound.
A program may use at most 128 MiB of HBM per device.

```python
import jax
import jax.numpy as jnp
from jax import lax

FR = 4
HALF = 16
HDIM = 128
HH = 64
WW = 32
CH = 1536
N_ROW = 4
N_COL = 2


def draw_queries(key, part):
    key = jax.random.fold_in(key, 11)
    drawn = jnp.clip(jax.random.normal(key, (FR, HH, WW, CH)), -6.0, 6.0)
    return drawn.astype(jnp.bfloat16)


def draw_keys(key, part):
    key = jax.random.fold_in(key, 23)
    drawn = jnp.clip(jax.random.normal(key, (FR, HH, WW, CH)), -6.0, 6.0)
    return drawn.astype(jnp.bfloat16)


def place_ends(drawn, stream_key, low, largest):
    longest = drawn.shape.index(max(drawn.shape))
    spots = []
    for shift in (0, 1):
        where = [jax.random.randint(jax.random.fold_in(stream_key, axis), (), 0, length) for axis, length in enumerate(drawn.shape)]
        where[longest] = (where[longest] + shift) % drawn.shape[longest]
        spots.append(tuple(where))
    return drawn.at[spots[0]].set(low).at[spots[1]].set(largest)


def levels(stream_key, extent, shards, smallest, top_value):
    loudness, own = 1.0, jax.random.fold_in(stream_key, 6)
    for dim, parts in shards:
        heights = jnp.exp(jax.random.uniform(jax.random.fold_in(own, dim), (parts,), jnp.float32, smallest / len(shards), top_value / len(shards)))
        loudness = loudness * jnp.repeat(heights, extent[dim] // parts).reshape([-1 if axis == dim else 1 for axis in range(len(extent))])
    return loudness


def gaussian(rng, extent, deviation, reach, pieces=(), kind=jnp.bfloat16):
    factor_of = levels(rng, extent, pieces, -0.22, 0.18) if pieces else 1.0
    result = jax.random.normal(rng, extent, jnp.float32) * deviation * factor_of
    return jnp.minimum(jnp.maximum(result, -reach), reach).astype(kind)


def setup_inputs(seed: int = 0, part: int = 0) -> dict:
    arg_keys = jax.random.split(jax.random.key(seed), 7)
    own_keys = jax.random.split(jax.random.fold_in(arg_keys[6], part), 7)
    return {
        "queries": draw_queries(jax.random.fold_in(jax.random.fold_in(arg_keys[6], part), 71), part),
        "keys": draw_keys(jax.random.fold_in(jax.random.fold_in(arg_keys[6], part), 71), part),
        "values": gaussian(own_keys[2], (FR, HH, WW, CH), 1.0, 6.0, ((1, 4), (2, 2), (3, 2))),
        "labels": place_ends(jax.random.randint(own_keys[3], (FR, N_ROW, N_COL), 0, 3), jax.random.fold_in(own_keys[3], 1), 0, 2).astype(jnp.int32),
        "pad_rows": jax.random.randint(own_keys[4], (1,), 0, 2 * HALF).astype(jnp.int32),
        "pad_cols": jax.random.randint(own_keys[5], (1,), 0, 2 * HALF).astype(jnp.int32),
    }


def attend(query_win, key_win, value_win, allowed):
    head_count = query_win.shape[1] // HDIM

    def one_head(head_index):
        first = head_index * HDIM
        query_head = lax.dynamic_slice_in_dim(query_win, first, HDIM, 1).astype(jnp.float32)
        key_head = lax.dynamic_slice_in_dim(key_win, first, HDIM, 1).astype(jnp.float32)
        value_head = lax.dynamic_slice_in_dim(value_win, first, HDIM, 1).astype(jnp.float32)
        scores = jnp.dot(query_head, key_head.T, precision=lax.Precision.HIGHEST) * HDIM ** -0.5
        scores = jnp.where(allowed, scores, -1e30)
        row_max = jnp.max(scores, axis=1, keepdims=True)
        exponent = jnp.exp(scores - row_max)
        weights = (exponent / jnp.sum(exponent, axis=1, keepdims=True)).astype(jnp.bfloat16)
        return jnp.dot(weights.astype(jnp.float32), value_head, precision=lax.Precision.HIGHEST).astype(jnp.bfloat16)

    heads_out = lax.map(one_head, jnp.arange(head_count, dtype=jnp.int32))
    return heads_out.transpose(1, 0, 2).reshape(query_win.shape[0], -1)


def reference(queries, keys, values, labels, pad_rows, pad_cols):
    frames, height, grid_width, channels = queries.shape
    row_ids = jnp.arange(height, dtype=jnp.int32)
    col_ids = jnp.arange(grid_width, dtype=jnp.int32)
    valid_mask = (row_ids[:, None] < height - pad_rows[0]) & (col_ids[None, :] < grid_width - pad_cols[0])
    valid_mask = jnp.broadcast_to(valid_mask[None], (frames, height, grid_width))
    token_labels = jnp.repeat(jnp.repeat(labels, HALF, axis=1), HALF, axis=2)
    win_rows = height // (2 * HALF)
    win_cols = grid_width // (2 * HALF)

    def to_windows(source):
        rolled = jnp.roll(source, (-HALF, -HALF), axis=(1, 2))
        rest = source.shape[3:]
        shaped = rolled.reshape((frames, win_rows, 2 * HALF, win_cols, 2 * HALF) + rest)
        order = (1, 3, 0, 2, 4) + tuple(range(5, 5 + len(rest)))
        return shaped.transpose(order).reshape((win_rows * win_cols, frames * 4 * HALF * HALF) + rest)

    def one_window(operands):
        query_win, key_win, value_win, label_win, valid_win = operands
        allowed = (label_win[:, None] == label_win[None, :]) & valid_win[None, :]
        return attend(query_win, key_win, value_win, allowed)

    outputs = lax.map(one_window, (to_windows(queries), to_windows(keys), to_windows(values), to_windows(token_labels), to_windows(valid_mask)))
    outputs = outputs.reshape(win_rows, win_cols, frames, 2 * HALF, 2 * HALF, channels)
    outputs = outputs.transpose(2, 0, 3, 1, 4, 5).reshape(frames, height, grid_width, channels)
    return jnp.roll(outputs, (HALF, HALF), axis=(1, 2))
```

```python
import functools
import math

import jax
import jax.numpy as jnp
from jax import lax
from jax.experimental import pallas as pl
from jax.experimental.pallas import tpu as pltpu
from jax.sharding import PartitionSpec as P

HDIM = 128
MESH = pl.DeviceIdType.MESH
MASKED = -1e30
SCALE = HDIM ** -0.5 * math.log2(math.e)
OWN, ROWS, COLS, DIAG = 0, 1, 2, 3
AHEAD = 2


def kernel(
    grid, sizes,
    q_hbm, k_hbm, v_hbm, labels, pad_rows, pad_cols, out_ref,
    q_buf, own, from_row, from_col, from_diag, bias, acc, top, total,
    local_sem, row_send, row_recv, col_send, col_recv, fwd_send, diag_recv,
):
    frames, half, width = grid
    n_row, n_col = sizes
    heads, tokens, _ = q_buf.shape
    block = half * width
    row = lax.axis_index("row")
    col = lax.axis_index("col")
    row2 = lax.rem(row + 2 * lax.rem(row, 2) - 1 + n_row, n_row)
    col2 = lax.rem(col + 2 * lax.rem(col, 2) - 1 + n_col, n_col)

    barrier = pltpu.get_barrier_semaphore()
    pl.semaphore_signal(barrier, inc=1, device_id={"row": row2}, device_id_type=MESH)
    pl.semaphore_signal(barrier, inc=1, device_id={"col": col2}, device_id_type=MESH)

    def lanes(h):
        return pl.ds(pl.multiple_of(h * HDIM, HDIM), HDIM)

    def local(h):
        sources = (k_hbm, v_hbm, q_hbm)
        targets = (own.at[0, h], own.at[1, h], q_buf.at[h])
        return [
            pltpu.make_async_copy(s.at[:, lanes(h)], t, local_sem.at[i, h])
            for i, (s, t) in enumerate(zip(sources, targets))
        ]

    def to_row(h):
        return [
            pltpu.make_async_remote_copy(
                s.at[:, lanes(h)], from_row.at[i, h], row_send.at[i, h], row_recv.at[i, h],
                device_id={"row": row2}, device_id_type=MESH)
            for i, s in enumerate((k_hbm, v_hbm))
        ]

    def to_col(h):
        return [
            pltpu.make_async_remote_copy(
                s.at[:, lanes(h)], from_col.at[i, h], col_send.at[i, h], col_recv.at[i, h],
                device_id={"col": col2}, device_id_type=MESH)
            for i, s in enumerate((k_hbm, v_hbm))
        ]

    def forward(h):
        return [
            pltpu.make_async_remote_copy(
                from_row.at[i, h], from_diag.at[i, h], fwd_send.at[i, h], diag_recv.at[i, h],
                device_id={"col": col2}, device_id_type=MESH)
            for i in range(2)
        ]

    def each(count, do):
        lax.fori_loop(0, count, lambda h, c: (do(h), c)[1], 0)

    def start_all(make):
        def do(h):
            for copy in make(h):
                copy.start()
        return do

    each(heads, start_all(local))
    pl.semaphore_wait(barrier, 2)
    each(AHEAD, start_all(lambda h: to_row(h) + to_col(h)))
    lax.fori_loop(AHEAD, heads, lambda h, c: (start_all(to_row)(h), c)[1], 0)

    token = lax.broadcasted_iota(jnp.int32, (1, tokens), 1)
    token_frame = token // block
    token_row = token % block // width
    token_col = token % width
    for slot, (r, c) in enumerate(((row, col), (row2, col), (row, col2), (row2, col2))):
        valid = (r * half + token_row < n_row * half - pad_rows[0]) & (
            c * width + token_col < n_col * width - pad_cols[0])
        key_label = jnp.full((1, tokens), labels[0, r, c], jnp.int32)
        for f in range(1, frames):
            key_label = jnp.where(token_frame == f, labels[f, r, c], key_label)
        for f in range(frames):
            allowed = valid & (key_label == labels[f, row, col])
            bias[pl.ds(slot * frames + f, 1), :] = jnp.where(allowed, 0.0, MASKED)

    def unit(slot, h, tile):
        k = tile[0, h]
        v = tile[1, h]
        for f in range(frames):
            rows = pl.ds(f * block, block)
            s = lax.dot_general(
                q_buf[h, rows, :], k, (((1,), (1,)), ((), ())),
                preferred_element_type=jnp.float32)
            s = s * SCALE + bias[pl.ds(slot * frames + f, 1), :]
            high = jnp.max(s, axis=1, keepdims=True)
            if slot != OWN:
                before = top[h, rows, :]
                high = jnp.maximum(high, before)
            p = jnp.exp2(s - high)
            sums = jnp.sum(p, axis=1, keepdims=True)
            part = jnp.dot(p.astype(jnp.bfloat16), v, preferred_element_type=jnp.float32)
            if slot != OWN:
                shrink = jnp.exp2(before - high)
                sums = sums + shrink * total[h, rows, :]
                part = part + shrink * acc[h, rows, :]
            if slot == DIAG:
                out_ref[rows, lanes(h)] = (part / sums).astype(out_ref.dtype)
            else:
                top[h, rows, :] = high
                total[h, rows, :] = sums
                acc[h, rows, :] = part

    def finish(h):
        for copy in forward(h):
            copy.wait_recv()
        unit(DIAG, h, from_diag)

    def step(h):
        for copy in local(h):
            copy.wait()
        unit(OWN, h, own)
        for arrived, onward in zip(to_row(h), forward(h)):
            arrived.wait_recv()
            onward.start()

        @pl.when(h + AHEAD < heads)
        def _():
            start_all(to_col)(h + AHEAD)

        unit(ROWS, h, from_row)
        for copy in to_col(h):
            copy.wait_recv()
        unit(COLS, h, from_col)

        @pl.when(h > 0)
        def _():
            finish(h - 1)

    each(heads, step)
    finish(heads - 1)

    def drain(h):
        for copy in to_row(h) + to_col(h) + forward(h):
            copy.wait_send()

    each(heads, drain)


def per_device(sizes, queries, keys, values, labels, pad_rows, pad_cols):
    frames, half, width, channels = queries.shape
    heads = channels // HDIM
    tokens = frames * half * width
    flat = (tokens, channels)
    tile = pltpu.VMEM((2, heads, tokens, HDIM), jnp.bfloat16)
    any_space = pl.BlockSpec(memory_space=pl.ANY)
    smem = pl.BlockSpec(memory_space=pltpu.SMEM)
    copies = pltpu.SemaphoreType.DMA((2, heads))
    out = pl.pallas_call(
        functools.partial(kernel, (frames, half, width), sizes),
        out_shape=jax.ShapeDtypeStruct(flat, queries.dtype),
        in_specs=[any_space] * 3 + [smem] * 3,
        out_specs=pl.BlockSpec(memory_space=pltpu.VMEM),
        scratch_shapes=[
            pltpu.VMEM((heads, tokens, HDIM), jnp.bfloat16),
            tile, tile, tile, tile,
            pltpu.VMEM((4 * frames, tokens), jnp.float32),
            pltpu.VMEM((heads, tokens, HDIM), jnp.float32),
            pltpu.VMEM((heads, tokens, 1), jnp.float32),
            pltpu.VMEM((heads, tokens, 1), jnp.float32),
            pltpu.SemaphoreType.DMA((3, heads)),
            copies, copies, copies, copies, copies, copies,
        ],
        compiler_params=pltpu.CompilerParams(
            collective_id=0, has_side_effects=True, vmem_limit_bytes=48 * 2 ** 20),
        cost_estimate=pl.CostEstimate(
            flops=16 * tokens * tokens * channels,
            bytes_accessed=8 * tokens * channels,
            transcendentals=4 * tokens * tokens * heads),
    )(queries.reshape(flat), keys.reshape(flat), values.reshape(flat), labels, pad_rows, pad_cols)
    return out.reshape(queries.shape)


def solution(mesh):
    placed = (
        P("grp", "row", "col", "hd"),
        P("grp", "row", "col", "hd"),
        P("grp", "row", "col", "hd"),
        P("grp", None, None),
        P("grp"),
        P("grp"),
    )
    return jax.shard_map(
        functools.partial(per_device, (mesh.shape["row"], mesh.shape["col"])),
        mesh=mesh,
        in_specs=placed,
        out_specs=P("grp", "row", "col", "hd"),
        check_vma=False,
    )
```

```python
import functools
import math

import jax
import jax.numpy as jnp
from jax import lax
from jax.experimental import pallas as pl
from jax.experimental.pallas import tpu as pltpu
from jax.sharding import PartitionSpec as P

HDIM = 128
MESH = pl.DeviceIdType.MESH
MASKED = -1e30
SCALE = HDIM ** -0.5 * math.log2(math.e)
OWN, ROWS, COLS, DIAG = 0, 1, 2, 3
LAG = 2


def kernel(
    grid, sizes,
    q_hbm, k_hbm, v_hbm, labels, pad_rows, pad_cols, out_ref,
    q_buf, own, from_row, from_col, from_diag, bias, acc, top, total,
    local_sem, row_send, row_recv, col_send, col_recv, fwd_send, diag_recv,
):
    frames, half, width = grid
    n_row, n_col = sizes
    heads, tokens, _ = q_buf.shape
    block = half * width
    row = lax.axis_index("row")
    col = lax.axis_index("col")
    row2 = lax.rem(row + 2 * lax.rem(row, 2) - 1 + n_row, n_row)
    col2 = lax.rem(col + 2 * lax.rem(col, 2) - 1 + n_col, n_col)

    barrier = pltpu.get_barrier_semaphore()
    pl.semaphore_signal(barrier, inc=1, device_id={"row": row2}, device_id_type=MESH)
    pl.semaphore_signal(barrier, inc=1, device_id={"col": col2}, device_id_type=MESH)

    def lanes(h):
        return pl.ds(pl.multiple_of(h * HDIM, HDIM), HDIM)

    def local(h):
        sources = (k_hbm, v_hbm, q_hbm)
        targets = (own.at[0, h], own.at[1, h], q_buf.at[h])
        return [
            pltpu.make_async_copy(s.at[:, lanes(h)], t, local_sem.at[i, h])
            for i, (s, t) in enumerate(zip(sources, targets))
        ]

    def to_row(h):
        return [
            pltpu.make_async_remote_copy(
                s.at[:, lanes(h)], from_row.at[i, h], row_send.at[i, h], row_recv.at[i, h],
                device_id={"row": row2}, device_id_type=MESH)
            for i, s in enumerate((k_hbm, v_hbm))
        ]

    def to_col(h):
        return [
            pltpu.make_async_remote_copy(
                s.at[:, lanes(h)], from_col.at[i, h], col_send.at[i, h], col_recv.at[i, h],
                device_id={"col": col2}, device_id_type=MESH)
            for i, s in enumerate((k_hbm, v_hbm))
        ]

    def forward(h):
        return [
            pltpu.make_async_remote_copy(
                from_row.at[i, h], from_diag.at[i, h], fwd_send.at[i, h], diag_recv.at[i, h],
                device_id={"col": col2}, device_id_type=MESH)
            for i in range(2)
        ]

    def each(count, do):
        lax.fori_loop(0, count, lambda h, c: (do(h), c)[1], 0)

    def start_all(make):
        def do(h):
            for copy in make(h):
                copy.start()
        return do

    each(heads, start_all(local))
    pl.semaphore_wait(barrier, 2)
    each(heads, start_all(lambda h: to_row(h) + to_col(h)))

    token = lax.broadcasted_iota(jnp.int32, (1, tokens), 1)
    token_frame = token // block
    token_row = token % block // width
    token_col = token % width
    for slot, (r, c) in enumerate(((row, col), (row2, col), (row, col2), (row2, col2))):
        valid = (r * half + token_row < n_row * half - pad_rows[0]) & (
            c * width + token_col < n_col * width - pad_cols[0])
        key_label = jnp.full((1, tokens), labels[0, r, c], jnp.int32)
        for f in range(1, frames):
            key_label = jnp.where(token_frame == f, labels[f, r, c], key_label)
        for f in range(frames):
            allowed = valid & (key_label == labels[f, row, col])
            bias[pl.ds(slot * frames + f, 1), :] = jnp.where(allowed, 0.0, MASKED)

    def unit(slot, h, tile):
        k = tile[0, h]
        v = tile[1, h]
        for f in range(frames):
            rows = pl.ds(f * block, block)
            s = lax.dot_general(
                q_buf[h, rows, :], k, (((1,), (1,)), ((), ())),
                preferred_element_type=jnp.float32)
            s = s * SCALE + bias[pl.ds(slot * frames + f, 1), :]
            high = jnp.max(s, axis=1, keepdims=True)
            if slot != OWN:
                before = top[h, rows, :]
                high = jnp.maximum(high, before)
            p = jnp.exp2(s - high)
            sums = jnp.sum(p, axis=1, keepdims=True)
            part = jnp.dot(p.astype(jnp.bfloat16), v, preferred_element_type=jnp.float32)
            if slot != OWN:
                shrink = jnp.exp2(before - high)
                sums = sums + shrink * total[h, rows, :]
                part = part + shrink * acc[h, rows, :]
            if slot == DIAG:
                out_ref[rows, lanes(h)] = (part / sums).astype(out_ref.dtype)
            else:
                top[h, rows, :] = high
                total[h, rows, :] = sums
                acc[h, rows, :] = part

    def finish(h):
        for copy in forward(h):
            copy.wait_recv()
        unit(DIAG, h, from_diag)

    def near(h):
        for copy in local(h):
            copy.wait()
        unit(OWN, h, own)

        @pl.when(h > 0)
        def _():
            column(h - 1)

    def column(h):
        for copy in to_col(h):
            copy.wait_recv()
        unit(COLS, h, from_col)

    def far(h):
        for arrived, onward in zip(to_row(h), forward(h)):
            arrived.wait_recv()
            onward.start()

        @pl.when(h == 0)
        def _():
            column(heads - 1)

        unit(ROWS, h, from_row)

        @pl.when(h >= LAG)
        def _():
            finish(h - LAG)

    each(heads, near)
    each(heads, far)
    lax.fori_loop(heads - LAG, heads, lambda h, c: (finish(h), c)[1], 0)

    def drain(h):
        for copy in to_row(h) + to_col(h) + forward(h):
            copy.wait_send()

    each(heads, drain)


def per_device(sizes, queries, keys, values, labels, pad_rows, pad_cols):
    frames, half, width, channels = queries.shape
    heads = channels // HDIM
    tokens = frames * half * width
    flat = (tokens, channels)
    tile = pltpu.VMEM((2, heads, tokens, HDIM), jnp.bfloat16)
    any_space = pl.BlockSpec(memory_space=pl.ANY)
    smem = pl.BlockSpec(memory_space=pltpu.SMEM)
    copies = pltpu.SemaphoreType.DMA((2, heads))
    out = pl.pallas_call(
        functools.partial(kernel, (frames, half, width), sizes),
        out_shape=jax.ShapeDtypeStruct(flat, queries.dtype),
        in_specs=[any_space] * 3 + [smem] * 3,
        out_specs=pl.BlockSpec(memory_space=pltpu.VMEM),
        scratch_shapes=[
            pltpu.VMEM((heads, tokens, HDIM), jnp.bfloat16),
            tile, tile, tile, tile,
            pltpu.VMEM((4 * frames, tokens), jnp.float32),
            pltpu.VMEM((heads, tokens, HDIM), jnp.float32),
            pltpu.VMEM((heads, tokens, 1), jnp.float32),
            pltpu.VMEM((heads, tokens, 1), jnp.float32),
            pltpu.SemaphoreType.DMA((3, heads)),
            copies, copies, copies, copies, copies, copies,
        ],
        compiler_params=pltpu.CompilerParams(
            collective_id=0, has_side_effects=True, vmem_limit_bytes=60 * 2 ** 20),
        cost_estimate=pl.CostEstimate(
            flops=16 * tokens * tokens * channels,
            bytes_accessed=8 * tokens * channels,
            transcendentals=4 * tokens * tokens * heads),
    )(queries.reshape(flat), keys.reshape(flat), values.reshape(flat), labels, pad_rows, pad_cols)
    return out.reshape(queries.shape)


def solution(mesh):
    placed = (
        P("grp", "row", "col", "hd"),
        P("grp", "row", "col", "hd"),
        P("grp", "row", "col", "hd"),
        P("grp", None, None),
        P("grp"),
        P("grp"),
    )
    return jax.shard_map(
        functools.partial(per_device, (mesh.shape["row"], mesh.shape["col"])),
        mesh=mesh,
        in_specs=placed,
        out_specs=P("grp", "row", "col", "hd"),
        check_vma=False,
    )
```

```python
import functools
import math

import jax
import jax.numpy as jnp
from jax import lax
from jax.experimental import pallas as pl
from jax.experimental.pallas import tpu as pltpu
from jax.sharding import PartitionSpec as P

HDIM = 128
MESH = pl.DeviceIdType.MESH
MASKED = -1e30
SCALE = HDIM ** -0.5 * math.log2(math.e)
OWN, ROWS, COLS, DIAG = 0, 1, 2, 3
PARTS = 2


def kernel(
    grid, sizes,
    q_hbm, k_hbm, v_hbm, labels_hbm, pad_rows, pad_cols, out_ref,
    q_buf, own, from_row, from_col, from_diag, bias, acc, top, total, labels, label_sem,
    local_sem, row_send, row_recv, col_send, col_recv, fwd_send, diag_recv,
):
    frames, half, width = grid
    n_row, n_col = sizes
    heads, tokens, _ = q_buf.shape
    block = half * width
    size = tokens // PARTS
    row = lax.axis_index("row")
    col = lax.axis_index("col")
    row2 = lax.rem(row + 2 * lax.rem(row, 2) - 1 + n_row, n_row)
    col2 = lax.rem(col + 2 * lax.rem(col, 2) - 1 + n_col, n_col)

    barrier = pltpu.get_barrier_semaphore()
    pl.semaphore_signal(barrier, inc=1, device_id={"row": row2}, device_id_type=MESH)
    pl.semaphore_signal(barrier, inc=1, device_id={"col": col2}, device_id_type=MESH)

    def lanes(h):
        return pl.ds(pl.multiple_of(h * HDIM, HDIM), HDIM)

    def piece(p):
        if p is None:
            return pl.ds(0, tokens)
        return pl.ds(p * size, size)

    def mark(p):
        return 0 if p is None else p

    def local(h):
        sources = (k_hbm, v_hbm, q_hbm)
        targets = (own.at[0, h], own.at[1, h], q_buf.at[h])
        return [
            pltpu.make_async_copy(s.at[:, lanes(h)], t, local_sem.at[i, h])
            for i, (s, t) in enumerate(zip(sources, targets))
        ]

    def to_row(h, p=None):
        return [
            pltpu.make_async_remote_copy(
                s.at[piece(p), lanes(h)], from_row.at[i, h, piece(p)],
                row_send.at[i, h, mark(p)], row_recv.at[i, h, mark(p)],
                device_id={"row": row2}, device_id_type=MESH)
            for i, s in enumerate((k_hbm, v_hbm))
        ]

    def to_col(h):
        return [
            pltpu.make_async_remote_copy(
                s.at[:, lanes(h)], from_col.at[i, h], col_send.at[i, h], col_recv.at[i, h],
                device_id={"col": col2}, device_id_type=MESH)
            for i, s in enumerate((k_hbm, v_hbm))
        ]

    def forward(h, p=None):
        return [
            pltpu.make_async_remote_copy(
                from_row.at[i, h, piece(p)], from_diag.at[i, h, piece(p)],
                fwd_send.at[i, h, mark(p)], diag_recv.at[i, h, mark(p)],
                device_id={"col": col2}, device_id_type=MESH)
            for i in range(2)
        ]

    def each(count, do):
        lax.fori_loop(0, count, lambda h, c: (do(h), c)[1], 0)

    def start_all(make):
        def do(h):
            for copy in make(h):
                copy.start()
        return do

    label_copy = pltpu.make_async_copy(labels_hbm, labels, label_sem)
    label_copy.start()
    each(heads, start_all(local))
    pl.semaphore_wait(barrier, 2)

    last = heads - 1
    each(last, start_all(lambda h: to_col(h) + to_row(h)))
    for part in range(PARTS):
        start_all(lambda h: to_row(h, part))(last)
    start_all(to_col)(last)

    label_copy.wait()
    token = lax.broadcasted_iota(jnp.int32, (1, tokens), 1)
    token_frame = token // block
    token_row = token % block // width
    token_col = token % width
    for slot, (r, c) in enumerate(((row, col), (row2, col), (row, col2), (row2, col2))):
        valid = (r * half + token_row < n_row * half - pad_rows[0]) & (
            c * width + token_col < n_col * width - pad_cols[0])
        key_label = jnp.full((1, tokens), labels[0, r, c], jnp.int32)
        for f in range(1, frames):
            key_label = jnp.where(token_frame == f, labels[f, r, c], key_label)
        for f in range(frames):
            allowed = valid & (key_label == labels[f, row, col])
            bias[pl.ds(slot * frames + f, 1), :] = jnp.where(allowed, 0.0, MASKED)

    def unit(slot, h, tile, part=None):
        start, count = (0, tokens) if part is None else (part * size, size)
        keys = pl.ds(start, count)
        k = tile[0, h, keys, :]
        v = tile[1, h, keys, :]
        for f in range(frames):
            rows = pl.ds(f * block, block)
            s = lax.dot_general(
                q_buf[h, rows, :], k, (((1,), (1,)), ((), ())),
                preferred_element_type=jnp.float32)
            s = s * SCALE + bias[pl.ds(slot * frames + f, 1), keys]
            high = jnp.max(s, axis=1, keepdims=True)
            if slot != OWN:
                before = top[h, rows, :]
                high = jnp.maximum(high, before)
            p = jnp.exp2(s - high)
            sums = jnp.sum(p, axis=1, keepdims=True)
            added = jnp.dot(p.astype(jnp.bfloat16), v, preferred_element_type=jnp.float32)
            if slot != OWN:
                shrink = jnp.exp2(before - high)
                sums = sums + shrink * total[h, rows, :]
                added = added + shrink * acc[h, rows, :]
            if slot == DIAG and part in (None, PARTS - 1):
                out_ref[rows, lanes(h)] = (added / sums).astype(out_ref.dtype)
            else:
                top[h, rows, :] = high
                total[h, rows, :] = sums
                acc[h, rows, :] = added

    def arrive(h, p=None):
        for copy in forward(h, p):
            copy.wait_recv()

    def finish(h):
        arrive(h)
        unit(DIAG, h, from_diag)

    def pass_on(h, p=None):
        for arrived, onward in zip(to_row(h, p), forward(h, p)):
            arrived.wait_recv()
            onward.start()

    def near(h):
        for copy in local(h):
            copy.wait()
        unit(OWN, h, own)

        @pl.when(h > 0)
        def _():
            column(h - 1)

    def column(h):
        for copy in to_col(h):
            copy.wait_recv()
        unit(COLS, h, from_col)

    def far(h):
        @pl.when(h >= 2)
        def _():
            finish(h - 2)

        pass_on(h)

        @pl.when(h == 0)
        def _():
            column(heads - 1)

        unit(ROWS, h, from_row)

    each(heads, near)
    each(last, far)
    finish(last - 2)
    for part in range(PARTS):
        pass_on(last, part)
        if part == 0:
            finish(last - 1)
        unit(ROWS, last, from_row, part)
    for part in range(PARTS):
        arrive(last, part)
        unit(DIAG, last, from_diag, part)

    def drain(h):
        for copy in to_row(h) + forward(h) + to_col(h):
            copy.wait_send()

    each(last, drain)
    for part in range(PARTS):
        for copy in to_row(last, part) + forward(last, part):
            copy.wait_send()
    for copy in to_col(last):
        copy.wait_send()


def per_device(sizes, queries, keys, values, labels, pad_rows, pad_cols):
    frames, half, width, channels = queries.shape
    heads = channels // HDIM
    tokens = frames * half * width
    flat = (tokens, channels)
    tile = pltpu.VMEM((2, heads, tokens, HDIM), jnp.bfloat16)
    any_space = pl.BlockSpec(memory_space=pltpu.HBM)
    smem = pl.BlockSpec(memory_space=pltpu.SMEM)
    copies = pltpu.SemaphoreType.DMA((2, heads))
    part_copies = pltpu.SemaphoreType.DMA((2, heads, PARTS))
    out = pl.pallas_call(
        functools.partial(kernel, (frames, half, width), sizes),
        out_shape=jax.ShapeDtypeStruct(flat, queries.dtype),
        in_specs=[any_space] * 4 + [smem] * 2,
        out_specs=pl.BlockSpec(memory_space=pltpu.VMEM),
        scratch_shapes=[
            pltpu.VMEM((heads, tokens, HDIM), jnp.bfloat16),
            tile, tile, tile, tile,
            pltpu.VMEM((4 * frames, tokens), jnp.float32),
            pltpu.VMEM((heads, tokens, HDIM), jnp.float32),
            pltpu.VMEM((heads, tokens, 1), jnp.float32),
            pltpu.VMEM((heads, tokens, 1), jnp.float32),
            pltpu.SMEM(labels.shape, jnp.int32),
            pltpu.SemaphoreType.DMA,
            pltpu.SemaphoreType.DMA((3, heads)),
            part_copies, part_copies, copies, copies, part_copies, part_copies,
        ],
        compiler_params=pltpu.CompilerParams(
            collective_id=0, has_side_effects=True, vmem_limit_bytes=48 * 2 ** 20),
        cost_estimate=pl.CostEstimate(
            flops=16 * tokens * tokens * channels,
            bytes_accessed=8 * tokens * channels,
            transcendentals=4 * tokens * tokens * heads),
    )(queries.reshape(flat), keys.reshape(flat), values.reshape(flat), labels, pad_rows, pad_cols)
    return out.reshape(queries.shape)


def solution(mesh):
    placed = (
        P("grp", "row", "col", "hd"),
        P("grp", "row", "col", "hd"),
        P("grp", "row", "col", "hd"),
        P("grp", None, None),
        P("grp"),
        P("grp"),
    )
    return jax.shard_map(
        functools.partial(per_device, (mesh.shape["row"], mesh.shape["col"])),
        mesh=mesh,
        in_specs=placed,
        out_specs=P("grp", "row", "col", "hd"),
        check_vma=False,
    )
```

```python
import functools
import math

import jax
import jax.numpy as jnp
from jax import lax
from jax.experimental import pallas as pl
from jax.experimental.pallas import tpu as pltpu
from jax.sharding import PartitionSpec as P

HDIM = 128
MESH = pl.DeviceIdType.MESH
MASKED = -1e30
SCALE = HDIM ** -0.5 * math.log2(math.e)
OWN, ROWS, COLS, DIAG = 0, 1, 2, 3
PARTS = 2


def kernel(
    grid, sizes,
    q_hbm, k_hbm, v_hbm, labels_hbm, pad_rows, pad_cols, out_ref,
    q_buf, own, from_row, from_col, from_diag, bias, acc, top, total, labels, label_sem,
    local_sem, row_send, row_recv, col_send, col_recv, fwd_send, diag_recv,
):
    frames, half, width = grid
    n_row, n_col = sizes
    heads, tokens, _ = q_buf.shape
    block = half * width
    size = tokens // PARTS
    row = lax.axis_index("row")
    col = lax.axis_index("col")
    row2 = lax.rem(row + 2 * lax.rem(row, 2) - 1 + n_row, n_row)
    col2 = lax.rem(col + 2 * lax.rem(col, 2) - 1 + n_col, n_col)

    barrier = pltpu.get_barrier_semaphore()
    pl.semaphore_signal(barrier, inc=1, device_id={"row": row2}, device_id_type=MESH)
    pl.semaphore_signal(barrier, inc=1, device_id={"col": col2}, device_id_type=MESH)

    def lanes(h):
        return pl.ds(pl.multiple_of(h * HDIM, HDIM), HDIM)

    def piece(p):
        if p is None:
            return pl.ds(0, tokens)
        return pl.ds(p * size, size)

    def mark(p):
        return 0 if p is None else p

    def local(h):
        sources = (k_hbm, v_hbm, q_hbm)
        targets = (own.at[0, h], own.at[1, h], q_buf.at[h])
        return [
            pltpu.make_async_copy(s.at[:, lanes(h)], t, local_sem.at[i, h])
            for i, (s, t) in enumerate(zip(sources, targets))
        ]

    def to_row(h, p=None):
        return [
            pltpu.make_async_remote_copy(
                s.at[piece(p), lanes(h)], from_row.at[i, h, piece(p)],
                row_send.at[i, h, mark(p)], row_recv.at[i, h, mark(p)],
                device_id={"row": row2}, device_id_type=MESH)
            for i, s in enumerate((k_hbm, v_hbm))
        ]

    def to_col(h):
        return [
            pltpu.make_async_remote_copy(
                s.at[:, lanes(h)], from_col.at[i, h], col_send.at[i, h], col_recv.at[i, h],
                device_id={"col": col2}, device_id_type=MESH)
            for i, s in enumerate((k_hbm, v_hbm))
        ]

    def forward(h, p=None):
        return [
            pltpu.make_async_remote_copy(
                from_row.at[i, h, piece(p)], from_diag.at[i, h, piece(p)],
                fwd_send.at[i, h, mark(p)], diag_recv.at[i, h, mark(p)],
                device_id={"col": col2}, device_id_type=MESH)
            for i in range(2)
        ]

    def each(count, do):
        lax.fori_loop(0, count, lambda h, c: (do(h), c)[1], 0)

    def start_all(make):
        def do(h):
            for copy in make(h):
                copy.start()
        return do

    label_copy = pltpu.make_async_copy(labels_hbm, labels, label_sem)
    label_copy.start()
    each(heads, start_all(local))
    pl.semaphore_wait(barrier, 2)

    last = heads - 1
    each(last, start_all(lambda h: to_col(h) + to_row(h)))
    for part in range(PARTS):
        start_all(lambda h: to_row(h, part))(last)
    start_all(to_col)(last)

    label_copy.wait()
    token = lax.broadcasted_iota(jnp.int32, (1, tokens), 1)
    token_frame = token // block
    token_row = token % block // width
    token_col = token % width
    for slot, (r, c) in enumerate(((row, col), (row2, col), (row, col2), (row2, col2))):
        valid = (r * half + token_row < n_row * half - pad_rows[0]) & (
            c * width + token_col < n_col * width - pad_cols[0])
        key_label = jnp.full((1, tokens), labels[0, r, c], jnp.int32)
        for f in range(1, frames):
            key_label = jnp.where(token_frame == f, labels[f, r, c], key_label)
        for f in range(frames):
            allowed = valid & (key_label == labels[f, row, col])
            bias[pl.ds(slot * frames + f, 1), :] = jnp.where(allowed, 0.0, MASKED)

    def unit(slot, h, tile, part=None):
        start, count = (0, tokens) if part is None else (part * size, size)
        keys = pl.ds(start, count)
        k = tile[0, h, keys, :]
        v = tile[1, h, keys, :]
        for f in range(frames):
            rows = pl.ds(f * block, block)
            s = lax.dot_general(
                q_buf[h, rows, :], k, (((1,), (1,)), ((), ())),
                preferred_element_type=jnp.float32)
            s = s * SCALE + bias[pl.ds(slot * frames + f, 1), keys]
            high = jnp.max(s, axis=1, keepdims=True)
            if slot != OWN:
                before = top[h, rows, :]
                high = jnp.maximum(high, before)
            p = jnp.exp2(s - high)
            sums = jnp.sum(p, axis=1, keepdims=True)
            added = jnp.dot(p.astype(jnp.bfloat16), v, preferred_element_type=jnp.float32)
            if slot != OWN:
                shrink = jnp.exp2(before - high)
                sums = sums + shrink * total[h, rows, :]
                added = added + shrink * acc[h, rows, :]
            if slot == DIAG and part in (None, PARTS - 1):
                out_ref[rows, lanes(h)] = (added / sums).astype(out_ref.dtype)
            else:
                top[h, rows, :] = high
                total[h, rows, :] = sums
                acc[h, rows, :] = added

    def arrive(h, p=None):
        for copy in forward(h, p):
            copy.wait_recv()

    def finish(h):
        arrive(h)
        unit(DIAG, h, from_diag)

    def pass_on(h, p=None):
        for arrived, onward in zip(to_row(h, p), forward(h, p)):
            arrived.wait_recv()
            onward.start()

    def near(h):
        for copy in local(h):
            copy.wait()
        unit(OWN, h, own)

        @pl.when(h > 0)
        def _():
            column(h - 1)

    def column(h):
        for copy in to_col(h):
            copy.wait_recv()
        unit(COLS, h, from_col)

    def far(h):
        @pl.when(h >= 2)
        def _():
            finish(h - 2)

        pass_on(h)

        @pl.when(h == 0)
        def _():
            column(heads - 1)

        unit(ROWS, h, from_row)

    each(heads, near)
    each(last, far)
    finish(last - 2)
    for part in range(PARTS):
        pass_on(last, part)
        if part == 0:
            finish(last - 1)
        unit(ROWS, last, from_row, part)
    for part in range(PARTS):
        arrive(last, part)
        unit(DIAG, last, from_diag, part)

    def drain(h):
        for copy in to_row(h) + forward(h) + to_col(h):
            copy.wait_send()

    each(last, drain)
    for part in range(PARTS):
        for copy in to_row(last, part) + forward(last, part):
            copy.wait_send()
    for copy in to_col(last):
        copy.wait_send()


def per_device(sizes, queries, keys, values, labels, pad_rows, pad_cols):
    frames, half, width, channels = queries.shape
    heads = channels // HDIM
    tokens = frames * half * width
    flat = (tokens, channels)
    tile = pltpu.VMEM((2, heads, tokens, HDIM), jnp.bfloat16)
    any_space = pl.BlockSpec(memory_space=pltpu.HBM)
    smem = pl.BlockSpec(memory_space=pltpu.SMEM)
    copies = pltpu.SemaphoreType.DMA((2, heads))
    part_copies = pltpu.SemaphoreType.DMA((2, heads, PARTS))
    out = pl.pallas_call(
        functools.partial(kernel, (frames, half, width), sizes),
        out_shape=jax.ShapeDtypeStruct(flat, queries.dtype),
        in_specs=[any_space] * 4 + [smem] * 2,
        out_specs=pl.BlockSpec(memory_space=pltpu.VMEM),
        scratch_shapes=[
            pltpu.VMEM((heads, tokens, HDIM), jnp.bfloat16),
            tile, tile, tile, tile,
            pltpu.VMEM((4 * frames, tokens), jnp.float32),
            pltpu.VMEM((heads, tokens, HDIM), jnp.float32),
            pltpu.VMEM((heads, tokens, 1), jnp.float32),
            pltpu.VMEM((heads, tokens, 1), jnp.float32),
            pltpu.SMEM(labels.shape, jnp.int32),
            pltpu.SemaphoreType.DMA,
            pltpu.SemaphoreType.DMA((3, heads)),
            part_copies, part_copies, copies, copies, part_copies, part_copies,
        ],
        compiler_params=pltpu.CompilerParams(
            collective_id=0, has_side_effects=True, vmem_limit_bytes=52 * 2 ** 20),
        cost_estimate=pl.CostEstimate(
            flops=16 * tokens * tokens * channels,
            bytes_accessed=8 * tokens * channels,
            transcendentals=4 * tokens * tokens * heads),
    )(queries.reshape(flat), keys.reshape(flat), values.reshape(flat), labels, pad_rows, pad_cols)
    return out.reshape(queries.shape)


def solution(mesh):
    placed = (
        P("grp", "row", "col", "hd"),
        P("grp", "row", "col", "hd"),
        P("grp", "row", "col", "hd"),
        P("grp", None, None),
        P("grp"),
        P("grp"),
    )
    return jax.shard_map(
        functools.partial(per_device, (mesh.shape["row"], mesh.shape["col"])),
        mesh=mesh,
        in_specs=placed,
        out_specs=P("grp", "row", "col", "hd"),
        check_vma=False,
    )
```
